128 devices in a mesh: gx: 8 (over x, core), gy: 16 (over z, y).
Axes of the slice: x: 4, y: 4, z: 4, core: 2. Of those that a mesh axis runs over, the one named last changes fastest.
Arguments:
- features: bfloat16 [524288, 128], P(('gx', 'gy')), may hold values from -6 to 6
- weight: bfloat16 [128, 128], replicated, may hold values from -0.5 to 0.5
- stripe_owner: int32 [8], replicated, may hold values from 0 to 127
- dense_vals: bfloat16 [128, 8, 32, 128, 128], P(('gx', 'gy')), may hold values from -0.12988281 to 0.12988281
- dense_rows: int32 [128, 8, 32], P(('gx', 'gy')), may hold values from 0 to 31
- dense_cols: int32 [128, 8, 32], P(('gx', 'gy')), may hold values from 0 to 31
- sparse_vals: bfloat16 [128, 256, 128, 128], P(('gx', 'gy')), may hold values from -0.12988281 to 0.12988281
- sparse_rows: int32 [128, 256], P(('gx', 'gy')), may hold values from 0 to 31
- sparse_cols: int32 [128, 256], P(('gx', 'gy')), may hold values from 0 to 255
- requests: int32 [128, 128, 256], P(('gx', 'gy')), may hold values from 0 to 4095
- counts: int32 [128, 128], P(('gx', 'gy')), may hold values from 192 to 256, as said below
Outputs:
- aggregated: bfloat16 [524288, 128], P(('gx', 'gy'))
The draws below stay inside these ranges and needn't reach their ends.
Inputs may be any that keep to these rules, and one draw needn't show every extreme that they name: Slots s >= counts[d, p] carry arbitrary row numbers and are not used; every requesting device has some owner with all 256 slots live.
All inputs are finite; a program needn't handle non-finite values.
Results may differ from the reference program's by a relative error of at most 0.0049.
Values may be sent and summed in bfloat16 or wider, within the bound.
No kernel may reach another device: no remote copies, remote signals or barrier semaphores. Data moves between devices by JAX's collectives and lax.ppermute only.
A program may use at most 192 MiB of HBM per device.

```python
import jax
import jax.numpy as jnp
from jax import lax

F = 128
TILE = 128
ROWS_DEV = 4096
ROUNDS = 8
DTILES = 32
STILES = 256
SLOTS = 256
NODES = 524288
RTILES = 32
SBLOCKS = 256
DEVICES = 128


def draw_counts(key, part):
    key = jax.random.fold_in(key, 7)
    key_base, key_full = jax.random.split(key, 2)
    short = jax.random.randint(key_base, (DEVICES, DEVICES), 0, SLOTS // 4 + 1)
    result = SLOTS - short
    full_owner = jax.random.randint(key_full, (DEVICES,), 0, DEVICES)
    result = result.at[jnp.arange(DEVICES), full_owner].set(SLOTS)
    return result.astype(jnp.int32)


def place_ends(drawn, own_key, least, largest):
    longest = drawn.shape.index(max(drawn.shape))
    spots = []
    for shift in (0, 1):
        where = [jax.random.randint(jax.random.fold_in(own_key, axis), (), 0, length) for axis, length in enumerate(drawn.shape)]
        where[longest] = (where[longest] + shift) % drawn.shape[longest]
        spots.append(tuple(where))
    return drawn.at[spots[0]].set(least).at[spots[1]].set(largest)


def steps_of(rng, extent, cuts, smallest, largest):
    loudness, own = 1.0, jax.random.fold_in(rng, 6)
    for axis_at, parts in cuts:
        steps = jnp.exp(jax.random.uniform(jax.random.fold_in(own, axis_at), (parts,), jnp.float32, smallest / len(cuts), largest / len(cuts)))
        loudness = loudness * jnp.repeat(steps, extent[axis_at] // parts).reshape([-1 if axis == axis_at else 1 for axis in range(len(extent))])
    return loudness


def noise(key, extent, spread, most, shards=(), held_as=jnp.bfloat16):
    drawn = spread * jax.random.normal(key, extent, jnp.float32)
    if shards:
        drawn = drawn * steps_of(key, extent, shards, -0.22, 0.18)
    return jnp.clip(drawn, -most, most).astype(held_as)


def setup_inputs(seed: int = 0) -> dict:
    splits = jax.random.split(jax.random.key(seed), 12)
    features = noise(splits[0], (NODES, F), 1.0, 6.0, ((0, 128),))
    weight = noise(splits[1], (F, F), F ** -0.5, 0.5)
    stripe_owner = place_ends(jax.random.randint(splits[2], (ROUNDS,), 0, DEVICES), jax.random.fold_in(splits[2], 1), 0, DEVICES - 1).astype(jnp.int32)
    dense_vals = noise(splits[3], (DEVICES, ROUNDS, DTILES, TILE, TILE), 0.022, 0.12988281, ((0, 128),))
    dense_rows = place_ends(jax.random.randint(splits[4], (DEVICES, ROUNDS, DTILES), 0, RTILES), jax.random.fold_in(splits[4], 1), 0, RTILES - 1).astype(jnp.int32)
    dense_cols = place_ends(jax.random.randint(splits[5], (DEVICES, ROUNDS, DTILES), 0, RTILES), jax.random.fold_in(splits[5], 1), 0, RTILES - 1).astype(jnp.int32)
    sparse_vals = noise(splits[6], (DEVICES, STILES, TILE, TILE), 0.022, 0.12988281, ((0, 128),))
    sparse_rows = place_ends(jax.random.randint(splits[7], (DEVICES, STILES), 0, RTILES), jax.random.fold_in(splits[7], 1), 0, RTILES - 1).astype(jnp.int32)
    sparse_cols = place_ends(jax.random.randint(splits[8], (DEVICES, STILES), 0, SBLOCKS), jax.random.fold_in(splits[8], 1), 0, SBLOCKS - 1).astype(jnp.int32)
    requests = place_ends(jax.random.randint(splits[9], (DEVICES, DEVICES, SLOTS), 0, ROWS_DEV), jax.random.fold_in(splits[9], 1), 0, ROWS_DEV - 1).astype(jnp.int32)
    counts = draw_counts(jax.random.fold_in(splits[11], 71), 0)
    return {"features": features, "weight": weight, "stripe_owner": stripe_owner, "dense_vals": dense_vals, "dense_rows": dense_rows, "dense_cols": dense_cols, "sparse_vals": sparse_vals, "sparse_rows": sparse_rows, "sparse_cols": sparse_cols, "requests": requests, "counts": counts}


def reference(features, weight, stripe_owner, dense_vals, dense_rows, dense_cols, sparse_vals, sparse_rows, sparse_cols, requests, counts):
    projected = jnp.dot(features, weight, preferred_element_type=jnp.float32).astype(jnp.bfloat16)
    row_tiles = ROWS_DEV // TILE
    tiled = projected.reshape(DEVICES, row_tiles, TILE, F)
    owner_blocks = tiled[stripe_owner]
    by_device = projected.reshape(DEVICES, ROWS_DEV, F)
    slot_index = jnp.arange(SLOTS, dtype=jnp.int32)
    owner_index = jnp.arange(DEVICES, dtype=jnp.int32)
    round_index = jnp.arange(ROUNDS, dtype=jnp.int32)

    def one_device(entry_list):
        dense_entries, dense_row_ids, dense_column_ids, sparse_entries, sparse_row_ids, sparse_column_ids, wanted_rows, active_mask = entry_list
        chosen = owner_blocks[round_index[:, None], dense_column_ids]
        dense_prod = jnp.einsum('rkij,rkjf->rkif', dense_entries.astype(jnp.float32), chosen.astype(jnp.float32))
        total = jnp.zeros((row_tiles, TILE, F), jnp.float32)
        total = total.at[dense_row_ids.reshape(-1)].add(dense_prod.reshape(-1, TILE, F))
        fetched = by_device[owner_index[:, None], wanted_rows]
        keep = (slot_index[None, :] < active_mask[:, None])[:, :, None]
        fetched = jnp.where(keep, fetched, jnp.zeros_like(fetched))
        selected_rows = fetched.reshape(-1, TILE, F)[sparse_column_ids]
        sparse_product = jnp.einsum('nbg,ngv->nbv', sparse_entries.astype(jnp.float32), selected_rows.astype(jnp.float32))
        total = total.at[sparse_row_ids].add(sparse_product)
        return jnp.maximum(total, 0.0).reshape(ROWS_DEV, F).astype(jnp.bfloat16)

    result = lax.map(one_device, (dense_vals, dense_rows, dense_cols, sparse_vals, sparse_rows, sparse_cols, requests, counts))
    return result.reshape(DEVICES * ROWS_DEV, F)
```

```python
import jax
import jax.numpy as jnp
from jax import lax
from jax.experimental import pallas as pl
from jax.experimental.pallas import tpu as pltpu
from jax.sharding import PartitionSpec as P

AXES = ("gx", "gy")
LEAD = 8
GROUP = 128
VMEM = 56 * 1024 * 1024


def gather_kernel(index_ref, table_ref, out_ref, wide_ref):
    nodes = table_ref.shape[0]
    count = out_ref.shape[0]
    base = pl.program_id(0) * count

    @pl.when(pl.program_id(0) == 0)
    def _():
        wide_ref[pl.ds(LEAD, nodes), :] = table_ref[...].astype(jnp.float32)
        wide_ref[pl.ds(LEAD + nodes, 8), :] = jnp.zeros((8, 128), jnp.float32)

    sublane = lax.broadcasted_iota(jnp.int32, (8, 128), 0)
    masks = [sublane == j for j in range(8)]

    def group(step, carry):
        start = pl.multiple_of(step * GROUP, GROUP)
        parts = []
        for eight in range(GROUP // 8):
            rows = None
            for j in range(8):
                at = index_ref[base + start + eight * 8 + j]
                found = wide_ref[pl.ds(at - j, 8), :]
                rows = found if rows is None else jnp.where(masks[j], found, rows)
            parts.append(rows)
        out_ref[pl.ds(start, GROUP), :] = jnp.concatenate(parts, axis=0).astype(jnp.bfloat16)
        return carry

    lax.fori_loop(0, count // GROUP, group, 0)


def gather_rows(wanted, projected, rows_step=2048):
    count = wanted.shape[0]
    nodes, width = projected.shape
    return pl.pallas_call(
        gather_kernel,
        grid_spec=pltpu.PrefetchScalarGridSpec(
            num_scalar_prefetch=1,
            grid=(count // rows_step,),
            in_specs=[pl.BlockSpec((nodes, width), lambda i, w: (0, 0))],
            out_specs=pl.BlockSpec((rows_step, width), lambda i, w: (i, 0)),
            scratch_shapes=[pltpu.VMEM((LEAD + nodes + 8, width), jnp.float32)],
        ),
        out_shape=jax.ShapeDtypeStruct((count, width), jnp.bfloat16),
        compiler_params=pltpu.CompilerParams(vmem_limit_bytes=VMEM),
        name="gather_rows",
    )(wanted, projected)


def dense_kernel(rows_ref, cols_ref, source_ref, values_ref, total_ref):
    step = pl.program_id(0)
    tiles = values_ref.shape[0]

    @pl.when(step == 0)
    def _():
        total_ref[...] = jnp.zeros_like(total_ref)

    stripe = step * tiles // 32
    for j in range(tiles):
        row = rows_ref[step * tiles + j]
        col = cols_ref[step * tiles + j]
        block = source_ref[pl.ds(col * 4, 4), stripe].reshape(128, 128)
        product = jnp.dot(values_ref[j], block, preferred_element_type=jnp.float32)
        at = pl.ds(pl.multiple_of(row * 128, 128), 128)
        total_ref[at, :] += product


def dense_sum(rows, cols, source, values, row_tiles, tiles=16):
    count = values.shape[0]
    return pl.pallas_call(
        dense_kernel,
        grid_spec=pltpu.PrefetchScalarGridSpec(
            num_scalar_prefetch=2,
            grid=(count // tiles,),
            in_specs=[
                pl.BlockSpec(source.shape, lambda i, r, c: (0, 0, 0, 0), pipeline_mode=pl.Buffered(1)),
                pl.BlockSpec((tiles, 128, 128), lambda i, r, c: (i, 0, 0)),
            ],
            out_specs=pl.BlockSpec((row_tiles * 128, 128), lambda i, r, c: (0, 0)),
        ),
        out_shape=jax.ShapeDtypeStruct((row_tiles * 128, 128), jnp.float32),
        compiler_params=pltpu.CompilerParams(vmem_limit_bytes=VMEM),
        name="dense_sum",
    )(rows, cols, source, values)


def sparse_kernel(rows_ref, cols_ref, source_ref, values_ref, begin_ref, out_ref, total_ref):
    step = pl.program_id(0)
    tiles = values_ref.shape[0]

    @pl.when(step == 0)
    def _():
        total_ref[...] = begin_ref[...]

    for j in range(tiles):
        row = rows_ref[step * tiles + j]
        col = cols_ref[step * tiles + j]
        block = source_ref[col]
        product = jnp.dot(values_ref[j], block, preferred_element_type=jnp.float32)
        at = pl.ds(pl.multiple_of(row * 128, 128), 128)
        total_ref[at, :] += product

    @pl.when(step == pl.num_programs(0) - 1)
    def _():
        out_ref[...] = jnp.maximum(total_ref[...], 0.0).astype(jnp.bfloat16)


def sparse_sum(rows, cols, source, values, begin, tiles=16):
    count = values.shape[0]
    return pl.pallas_call(
        sparse_kernel,
        grid_spec=pltpu.PrefetchScalarGridSpec(
            num_scalar_prefetch=2,
            grid=(count // tiles,),
            in_specs=[
                pl.BlockSpec(source.shape, lambda i, r, c: (0, 0, 0), pipeline_mode=pl.Buffered(1)),
                pl.BlockSpec((tiles, 128, 128), lambda i, r, c: (i, 0, 0)),
                pl.BlockSpec(begin.shape, lambda i, r, c: (0, 0), pipeline_mode=pl.Buffered(1)),
            ],
            out_specs=pl.BlockSpec(begin.shape, lambda i, r, c: (0, 0)),
            scratch_shapes=[pltpu.VMEM(begin.shape, jnp.float32)],
        ),
        out_shape=jax.ShapeDtypeStruct(begin.shape, jnp.bfloat16),
        compiler_params=pltpu.CompilerParams(vmem_limit_bytes=VMEM),
        name="sparse_sum",
    )(rows, cols, source, values, begin)


def local(
    features,
    weight,
    stripe_owner,
    dense_vals,
    dense_rows,
    dense_cols,
    sparse_vals,
    sparse_rows,
    sparse_cols,
    requests,
    counts,
):
    rows_dev, width = features.shape
    tile = dense_vals.shape[-1]
    row_tiles = rows_dev // tile
    owners = requests.shape[1]
    slots = requests.shape[2]
    piece = rows_dev // owners
    live = jnp.arange(slots, dtype=jnp.int32)[None, :] < counts[0][:, None]
    asked = jnp.where(live, requests[0] + LEAD, rows_dev + LEAD).reshape(owners, slots // width, width)
    projected = jnp.dot(features, weight, preferred_element_type=jnp.float32).astype(jnp.bfloat16)
    message = jnp.concatenate(
        [
            projected.reshape(owners, piece, width),
            (asked // 128).astype(jnp.bfloat16),
            (asked % 128).astype(jnp.bfloat16),
        ],
        axis=1,
    )
    message = lax.all_to_all(message, AXES, split_axis=0, concat_axis=0, tiled=True)
    digits = message[:, piece:].astype(jnp.int32).reshape(owners, 2, slots)
    wanted = (digits[:, 0] * 128 + digits[:, 1]).reshape(-1)
    mine = jnp.take(message[:, :piece], stripe_owner, axis=0)
    stripes = lax.all_gather(mine[None], AXES, axis=0, tiled=True)
    selected = gather_rows(wanted, projected).reshape(owners, slots, width)
    received = lax.all_to_all(selected, AXES, split_axis=0, concat_axis=0, tiled=True)
    total = dense_sum(
        dense_rows.reshape(-1), dense_cols.reshape(-1), stripes, dense_vals.reshape(-1, tile, tile), row_tiles
    )
    return sparse_sum(
        sparse_rows.reshape(-1), sparse_cols.reshape(-1), received.reshape(-1, tile, width), sparse_vals[0], total
    )


def solution(mesh):
    placed = (
        P(AXES, None),
        P(),
        P(),
        P(AXES, None, None, None, None),
        P(AXES, None, None),
        P(AXES, None, None),
        P(AXES, None, None, None),
        P(AXES, None),
        P(AXES, None),
        P(AXES, None, None),
        P(AXES, None),
    )
    return jax.shard_map(
        local, mesh=mesh, in_specs=placed, out_specs=P(AXES, None), check_vma=False
    )
```

```python
import functools

import jax
import jax.numpy as jnp
from jax import lax
from jax.experimental import pallas as pl
from jax.experimental.pallas import tpu as pltpu
from jax.sharding import PartitionSpec as P

AXES = ("gx", "gy")
LEAD = 8
VMEM = 56 * 1024 * 1024
UNROLL = 8
LOADS = 8


def gather_kernel(index_ref, table_ref, out_ref, wide_ref, *, half, halves):
    nodes = table_ref.shape[0]
    owners, tile, width = out_ref.shape
    first = pl.program_id(0) * owners

    @pl.when(pl.program_id(0) == 0)
    def _():
        wide_ref[pl.ds(LEAD, nodes), :] = table_ref[...].astype(jnp.float32)
        wide_ref[pl.ds(LEAD + nodes, 8), :] = jnp.zeros((8, width), jnp.float32)

    sublane = lax.broadcasted_iota(jnp.int32, (8, width), 0)
    masks = [sublane == j for j in range(8)]

    def one_owner(owner, carry):
        start = ((first + owner) * halves + half) * tile
        parts = []
        for eight in range(tile // 8):
            rows = None
            for j in range(8):
                at = index_ref[start + eight * 8 + j]
                found = wide_ref[pl.ds(at - j, 8), :]
                rows = found if rows is None else jnp.where(masks[j], found, rows)
            parts.append(rows)
        out_ref[owner] = jnp.concatenate(parts, axis=0).astype(jnp.bfloat16)
        return carry

    lax.fori_loop(0, owners, one_owner, 0)


def gather_rows(wanted, projected, half, halves, owners, owners_step=16):
    nodes, width = projected.shape
    tile = wanted.shape[0] // owners // halves
    return pl.pallas_call(
        functools.partial(gather_kernel, half=half, halves=halves),
        grid_spec=pltpu.PrefetchScalarGridSpec(
            num_scalar_prefetch=1,
            grid=(owners // owners_step,),
            in_specs=[pl.BlockSpec((nodes, width), lambda i, w: (0, 0))],
            out_specs=pl.BlockSpec((owners_step, tile, width), lambda i, w: (i, 0, 0)),
            scratch_shapes=[pltpu.VMEM((LEAD + nodes + 8, width), jnp.float32)],
        ),
        out_shape=jax.ShapeDtypeStruct((owners, tile, width), jnp.bfloat16),
        compiler_params=pltpu.CompilerParams(vmem_limit_bytes=VMEM),
        name="gather_rows",
    )(wanted, projected)


def value_copy(values_ref, held_ref, sems, part):
    size = held_ref.shape[0] // LOADS
    at = pl.ds(part * size, size)
    return pltpu.make_async_copy(values_ref.at[at], held_ref.at[at], sems.at[part])


def dense_kernel(
    rows_ref, cols_ref, source_hbm, values_ref, begin_ref, total_ref, source_ref, held_ref, sems, value_sems
):
    load_source = pltpu.make_async_copy(source_hbm, source_ref, sems.at[0])
    load_begin = pltpu.make_async_copy(begin_ref, total_ref, sems.at[1])
    load_source.start()
    load_begin.start()
    for part in range(LOADS):
        value_copy(values_ref, held_ref, value_sems, part).start()
    load_begin.wait()
    load_source.wait()
    count, tile, _ = held_ref.shape
    size = count // LOADS
    pieces, stripes, piece, _ = source_ref.shape
    per_tile = tile // piece

    def group(step, carry):
        @pl.when(step % (size // UNROLL) == 0)
        def _():
            value_copy(values_ref, held_ref, value_sems, step // (size // UNROLL)).wait()

        stripe = step // (count // stripes // UNROLL)
        for j in range(UNROLL):
            k = step * UNROLL + j
            block = source_ref[pl.ds(cols_ref[k] * per_tile, per_tile), stripe].reshape(tile, tile)
            product = jnp.dot(held_ref[k], block, preferred_element_type=jnp.float32)
            at = pl.ds(pl.multiple_of(rows_ref[k] * tile, tile), tile)
            total_ref[at, :] += product
        return carry

    lax.fori_loop(0, count // UNROLL, group, 0)


def dense_sum(rows, cols, source, values, begin):
    hbm = pl.BlockSpec(memory_space=pl.ANY)
    return pl.pallas_call(
        dense_kernel,
        grid_spec=pltpu.PrefetchScalarGridSpec(
            num_scalar_prefetch=2,
            grid=(1,),
            in_specs=[hbm] * 3,
            out_specs=pl.BlockSpec(begin.shape, lambda i, r, c: (0, 0)),
            scratch_shapes=[
                pltpu.VMEM(source.shape, jnp.bfloat16),
                pltpu.VMEM(values.shape, jnp.bfloat16),
                pltpu.SemaphoreType.DMA((2,)),
                pltpu.SemaphoreType.DMA((LOADS,)),
            ],
        ),
        out_shape=jax.ShapeDtypeStruct(begin.shape, jnp.float32),
        compiler_params=pltpu.CompilerParams(vmem_limit_bytes=VMEM),
        name="dense_sum",
    )(rows, cols, source, values, begin)


def sparse_kernel(rows_ref, cols_ref, source_hbm, values_ref, *refs, half, halves, last):
    out_ref, source_ref, held_ref, total_ref, list_ref, sems, value_sems = refs[-7:]
    nodes = out_ref.shape[0]
    count = held_ref.shape[0]
    load_source = pltpu.make_async_copy(source_hbm, source_ref, sems.at[0])
    load_source.start()
    if last:
        load_begin = pltpu.make_async_copy(refs[0], total_ref.at[pl.ds(0, nodes)], sems.at[1])
        load_begin.start()
    else:
        total_ref[...] = jnp.zeros_like(total_ref)
    for part in range(LOADS):
        value_copy(values_ref, held_ref, value_sems, part).start()

    def choose(k, taken):
        list_ref[taken] = k
        return taken + jnp.where(cols_ref[k] % halves == half, 1, 0)

    taken = lax.fori_loop(0, count, choose, 0, unroll=8)
    load_source.wait()
    if last:
        load_begin.wait()
    size = count // LOADS

    def wait_part(part, carry):
        value_copy(values_ref, held_ref, value_sems, part).wait()
        return carry

    def group(step, ready):
        last_k = list_ref[jnp.minimum(step * UNROLL + UNROLL, taken) - 1]
        need = last_k // size + 1
        lax.fori_loop(ready, need, wait_part, 0)
        for j in range(UNROLL):
            entry = step * UNROLL + j
            real = entry < taken
            k = jnp.where(real, list_ref[jnp.minimum(entry, taken - 1)], last_k)
            row = jnp.where(real, rows_ref[k], nodes // 128)
            block = source_ref[cols_ref[k] // halves]
            product = jnp.dot(held_ref[k], block, preferred_element_type=jnp.float32)
            at = pl.ds(pl.multiple_of(row * 128, 128), 128)
            total_ref[at, :] += product
        return jnp.maximum(ready, need)

    ready = lax.fori_loop(0, pl.cdiv(taken, UNROLL), group, 0)
    lax.fori_loop(ready, LOADS, wait_part, 0)
    result = total_ref[pl.ds(0, nodes), :]
    if last:
        result = jnp.maximum(result, 0.0)
    out_ref[...] = result.astype(out_ref.dtype)


def sparse_sum(rows, cols, source, values, nodes, half, halves, begin=None):
    hbm = pl.BlockSpec(memory_space=pl.ANY)
    shape = (nodes, source.shape[-1])
    last = begin is not None
    more = [begin] if last else []
    return pl.pallas_call(
        functools.partial(sparse_kernel, half=half, halves=halves, last=last),
        grid_spec=pltpu.PrefetchScalarGridSpec(
            num_scalar_prefetch=2,
            grid=(1,),
            in_specs=[hbm] * (2 + len(more)),
            out_specs=pl.BlockSpec(shape, lambda i, r, c: (0, 0)),
            scratch_shapes=[
                pltpu.VMEM(source.shape, jnp.bfloat16),
                pltpu.VMEM(values.shape, jnp.bfloat16),
                pltpu.VMEM((nodes + 128, shape[1]), jnp.float32),
                pltpu.SMEM((values.shape[0] + 8,), jnp.int32),
                pltpu.SemaphoreType.DMA((2,)),
                pltpu.SemaphoreType.DMA((LOADS,)),
            ],
        ),
        out_shape=jax.ShapeDtypeStruct(shape, jnp.bfloat16 if last else jnp.float32),
        compiler_params=pltpu.CompilerParams(vmem_limit_bytes=VMEM),
        name="sparse_sum",
    )(rows, cols, source, values, *more)


def local(
    features,
    weight,
    stripe_owner,
    dense_vals,
    dense_rows,
    dense_cols,
    sparse_vals,
    sparse_rows,
    sparse_cols,
    requests,
    counts,
):
    rows_dev, width = features.shape
    tile = dense_vals.shape[-1]
    owners = requests.shape[1]
    slots = requests.shape[2]
    halves = slots // tile
    piece = rows_dev // owners
    projected = jnp.dot(features, weight, preferred_element_type=jnp.float32).astype(jnp.bfloat16)
    pieces = lax.all_to_all(
        projected.reshape(owners, piece, width), AXES, split_axis=0, concat_axis=0, tiled=True
    )
    mine = jnp.take(pieces, stripe_owner, axis=0)
    live = jnp.arange(slots, dtype=jnp.int32)[None, :] < counts[0][:, None]
    asked = jnp.where(live, requests[0] + LEAD, rows_dev + LEAD)
    asked, mine = lax.optimization_barrier((asked, mine))
    stripes = lax.all_gather(mine[None], AXES, axis=0, tiled=True)
    wanted = lax.all_to_all(asked, AXES, split_axis=0, concat_axis=0, tiled=True).reshape(-1)
    selected = gather_rows(wanted, projected, 0, halves, owners)
    selected, wanted = lax.optimization_barrier((selected, wanted))
    received = lax.all_to_all(selected, AXES, split_axis=0, concat_axis=0, tiled=True)
    selected = gather_rows(wanted, projected, 1, halves, owners)
    total = sparse_sum(sparse_rows[0], sparse_cols[0], received, sparse_vals[0], rows_dev, 0, halves)
    received = lax.all_to_all(selected, AXES, split_axis=0, concat_axis=0, tiled=True)
    total = dense_sum(
        dense_rows.reshape(-1), dense_cols.reshape(-1), stripes, dense_vals.reshape(-1, tile, tile), total
    )
    return sparse_sum(sparse_rows[0], sparse_cols[0], received, sparse_vals[0], rows_dev, 1, halves, total)


def solution(mesh):
    lead = lambda rank: P(AXES, *([None] * (rank - 1)))
    placed = (
        lead(2), P(), P(), lead(5), lead(3), lead(3), lead(4), lead(2), lead(2), lead(3), lead(2),
    )
    return jax.shard_map(local, mesh=mesh, in_specs=placed, out_specs=lead(2), check_vma=False)
```

```python
import functools

import jax
import jax.numpy as jnp
from jax import lax
from jax.experimental import pallas as pl
from jax.experimental.pallas import tpu as pltpu
from jax.sharding import PartitionSpec as P

AXES = ("gx", "gy")
LEAD = 8
VMEM = 56 * 1024 * 1024
UNROLL = 32
LOADS = 4
EARLY = 24


def gather_kernel(index_ref, features_ref, weight_ref, *refs, half, halves, first_owner):
    out_ref, wide_ref = refs[-2:]
    nodes = features_ref.shape[0]
    owners, tile, width = out_ref.shape
    first = first_owner + pl.program_id(0) * owners

    @pl.when(pl.program_id(0) == 0)
    def _():
        projected = jnp.dot(features_ref[...], weight_ref[...], preferred_element_type=jnp.float32)
        wide_ref[pl.ds(LEAD, nodes), :] = projected.astype(jnp.bfloat16).astype(jnp.float32)
        wide_ref[pl.ds(LEAD + nodes, 8), :] = jnp.zeros((8, width), jnp.float32)

    sublane = lax.broadcasted_iota(jnp.int32, (8, width), 0)
    masks = [sublane == j for j in range(8)]

    def one_owner(owner, carry):
        start = ((first + owner) * halves + half) * tile
        parts = []
        for eight in range(tile // 8):
            rows = None
            for j in range(8):
                at = index_ref[start + eight * 8 + j]
                found = wide_ref[pl.ds(at - j, 8), :]
                rows = found if rows is None else jnp.where(masks[j], found, rows)
            parts.append(rows)
        out_ref[owner] = jnp.concatenate(parts, axis=0).astype(jnp.bfloat16)
        return carry

    lax.fori_loop(0, owners, one_owner, 0)


def gather_rows(wanted, features, weight, half, halves, owners, begin, end, earlier=None, owners_step=8):
    nodes, width = features.shape
    tile = wanted.shape[0] // owners // halves
    first = begin // owners_step
    more = [] if earlier is None else [earlier]
    return pl.pallas_call(
        functools.partial(gather_kernel, half=half, halves=halves, first_owner=begin),
        grid_spec=pltpu.PrefetchScalarGridSpec(
            num_scalar_prefetch=1,
            grid=((end - begin) // owners_step,),
            in_specs=[
                pl.BlockSpec((nodes, width), lambda i, w: (0, 0)),
                pl.BlockSpec((width, width), lambda i, w: (0, 0)),
            ]
            + [pl.BlockSpec(memory_space=pl.ANY) for _ in more],
            out_specs=pl.BlockSpec((owners_step, tile, width), lambda i, w: (first + i, 0, 0)),
            scratch_shapes=[pltpu.VMEM((LEAD + nodes + 8, width), jnp.float32)],
        ),
        out_shape=jax.ShapeDtypeStruct((owners, tile, width), jnp.bfloat16),
        input_output_aliases={3: 0} if more else {},
        compiler_params=pltpu.CompilerParams(vmem_limit_bytes=VMEM),
        name="gather_rows",
    )(wanted, features, weight, *more)


def value_copy(values_ref, held_ref, sems, part):
    size = held_ref.shape[0] // LOADS
    at = pl.ds(part * size, size)
    return pltpu.make_async_copy(values_ref.at[at], held_ref.at[at], sems.at[part])


def dense_kernel(
    rows_ref, cols_ref, source_hbm, values_ref, begin_hbm, total_ref, source_ref, held_ref, begin_ref, sems, value_sems
):
    load_source = pltpu.make_async_copy(source_hbm, source_ref, sems.at[0])
    load_begin = pltpu.make_async_copy(begin_hbm, begin_ref, sems.at[1])
    load_source.start()
    for part in range(LOADS):
        value_copy(values_ref, held_ref, value_sems, part).start()
    load_begin.start()
    total_ref[...] = jnp.zeros_like(total_ref)
    load_source.wait()
    count, tile, _ = held_ref.shape
    size = count // LOADS
    pieces, stripes, piece, _ = source_ref.shape
    per_tile = tile // piece

    def group(step, carry):
        @pl.when(step % (size // UNROLL) == 0)
        def _():
            value_copy(values_ref, held_ref, value_sems, step // (size // UNROLL)).wait()

        stripe = step // (count // stripes // UNROLL)
        for j in range(UNROLL):
            k = step * UNROLL + j
            block = source_ref[pl.ds(cols_ref[k] * per_tile, per_tile), stripe].reshape(tile, tile)
            product = jnp.dot(held_ref[k], block, preferred_element_type=jnp.float32)
            at = pl.ds(pl.multiple_of(rows_ref[k] * tile, tile), tile)
            total_ref[at, :] += product
        return carry

    lax.fori_loop(0, count // UNROLL, group, 0)
    load_begin.wait()
    total_ref[...] += begin_ref[...]


def dense_sum(rows, cols, source, values, begin):
    hbm = pl.BlockSpec(memory_space=pl.ANY)
    return pl.pallas_call(
        dense_kernel,
        grid_spec=pltpu.PrefetchScalarGridSpec(
            num_scalar_prefetch=2,
            grid=(1,),
            in_specs=[hbm] * 3,
            out_specs=pl.BlockSpec(begin.shape, lambda i, r, c: (0, 0)),
            scratch_shapes=[
                pltpu.VMEM(source.shape, jnp.bfloat16),
                pltpu.VMEM(values.shape, jnp.bfloat16),
                pltpu.VMEM(begin.shape, jnp.float32),
                pltpu.SemaphoreType.DMA((2,)),
                pltpu.SemaphoreType.DMA((LOADS,)),
            ],
        ),
        out_shape=jax.ShapeDtypeStruct(begin.shape, jnp.float32),
        compiler_params=pltpu.CompilerParams(vmem_limit_bytes=VMEM),
        name="dense_sum",
    )(rows, cols, source, values, begin)


def sparse_kernel(rows_ref, cols_ref, source_hbm, values_ref, *refs, half, halves, last):
    out_ref, source_ref, held_ref, total_ref, begin_ref, list_ref, sems, value_sems = refs[-8:]
    nodes = out_ref.shape[0]
    count = held_ref.shape[0]
    load_source = pltpu.make_async_copy(source_hbm, source_ref, sems.at[0])
    load_source.start()
    for part in range(LOADS):
        value_copy(values_ref, held_ref, value_sems, part).start()
    if last:
        load_begin = pltpu.make_async_copy(refs[0], begin_ref, sems.at[1])
        load_begin.start()
    total_ref[...] = jnp.zeros_like(total_ref)

    def choose(k, taken):
        list_ref[taken] = k
        return taken + jnp.where(cols_ref[k] % halves == half, 1, 0)

    taken = lax.fori_loop(0, count, choose, 0, unroll=8)
    load_source.wait()
    size = count // LOADS

    def wait_part(part, carry):
        value_copy(values_ref, held_ref, value_sems, part).wait()
        return carry

    def group(step, ready):
        last_k = list_ref[jnp.minimum(step * UNROLL + UNROLL, taken) - 1]
        need = last_k // size + 1
        lax.fori_loop(ready, need, wait_part, 0)
        for j in range(UNROLL):
            entry = step * UNROLL + j
            real = entry < taken
            k = jnp.where(real, list_ref[jnp.minimum(entry, taken - 1)], last_k)
            row = jnp.where(real, rows_ref[k], nodes // 128)
            block = source_ref[cols_ref[k] // halves]
            product = jnp.dot(held_ref[k], block, preferred_element_type=jnp.float32)
            at = pl.ds(pl.multiple_of(row * 128, 128), 128)
            total_ref[at, :] += product
        return jnp.maximum(ready, need)

    ready = lax.fori_loop(0, pl.cdiv(taken, UNROLL), group, 0)
    lax.fori_loop(ready, LOADS, wait_part, 0)
    result = total_ref[pl.ds(0, nodes), :]
    if last:
        load_begin.wait()
        result = jnp.maximum(result + begin_ref[...], 0.0)
    out_ref[...] = result.astype(out_ref.dtype)


def sparse_sum(rows, cols, source, values, nodes, half, halves, begin=None):
    hbm = pl.BlockSpec(memory_space=pl.ANY)
    shape = (nodes, source.shape[-1])
    last = begin is not None
    more = [begin] if last else []
    return pl.pallas_call(
        functools.partial(sparse_kernel, half=half, halves=halves, last=last),
        grid_spec=pltpu.PrefetchScalarGridSpec(
            num_scalar_prefetch=2,
            grid=(1,),
            in_specs=[hbm] * (2 + len(more)),
            out_specs=pl.BlockSpec(shape, lambda i, r, c: (0, 0)),
            scratch_shapes=[
                pltpu.VMEM(source.shape, jnp.bfloat16),
                pltpu.VMEM(values.shape, jnp.bfloat16),
                pltpu.VMEM((nodes + 128, shape[1]), jnp.float32),
                pltpu.VMEM(shape if last else (8, shape[1]), jnp.float32),
                pltpu.SMEM((values.shape[0] + 8,), jnp.int32),
                pltpu.SemaphoreType.DMA((2,)),
                pltpu.SemaphoreType.DMA((LOADS,)),
            ],
        ),
        out_shape=jax.ShapeDtypeStruct(shape, jnp.bfloat16 if last else jnp.float32),
        compiler_params=pltpu.CompilerParams(vmem_limit_bytes=VMEM),
        name="sparse_sum",
    )(rows, cols, source, values, *more)


def local(
    features,
    weight,
    stripe_owner,
    dense_vals,
    dense_rows,
    dense_cols,
    sparse_vals,
    sparse_rows,
    sparse_cols,
    requests,
    counts,
):
    rows_dev, width = features.shape
    tile = dense_vals.shape[-1]
    owners = requests.shape[1]
    slots = requests.shape[2]
    halves = slots // tile
    piece = rows_dev // owners
    live = jnp.arange(slots, dtype=jnp.int32)[None, :] < counts[0][:, None]
    asked = jnp.where(live, requests[0] + LEAD, rows_dev + LEAD).reshape(owners, halves, tile)
    message = jnp.concatenate(
        [
            features.reshape(owners, piece, width),
            (asked // 128).astype(jnp.bfloat16),
            (asked % 128).astype(jnp.bfloat16),
        ],
        axis=1,
    )
    message = lax.all_to_all(message, AXES, split_axis=0, concat_axis=0, tiled=True)
    mine = jnp.take(message[:, :piece], stripe_owner, axis=0)
    mine = jnp.dot(mine, weight, preferred_element_type=jnp.float32).astype(jnp.bfloat16)
    stripes = lax.all_gather(mine[None], AXES, axis=0, tiled=True)
    digits = message[:, piece:].astype(jnp.int32).reshape(owners, 2, slots)
    wanted = (digits[:, 0] * 128 + digits[:, 1]).reshape(-1)
    selected = gather_rows(wanted, features, weight, 0, halves, owners, 0, owners)
    if EARLY:
        ahead = gather_rows(wanted, features, weight, 1, halves, owners, 0, EARLY)
        selected, wanted, ahead = lax.optimization_barrier((selected, wanted, ahead))
    else:
        ahead = None
        selected, wanted = lax.optimization_barrier((selected, wanted))
    received = lax.all_to_all(selected, AXES, split_axis=0, concat_axis=0, tiled=True)
    selected = gather_rows(wanted, features, weight, 1, halves, owners, EARLY, owners, ahead)
    total = sparse_sum(sparse_rows[0], sparse_cols[0], received, sparse_vals[0], rows_dev, 0, halves)
    received = lax.all_to_all(selected, AXES, split_axis=0, concat_axis=0, tiled=True)
    total = dense_sum(
        dense_rows.reshape(-1), dense_cols.reshape(-1), stripes, dense_vals.reshape(-1, tile, tile), total
    )
    return sparse_sum(sparse_rows[0], sparse_cols[0], received, sparse_vals[0], rows_dev, 1, halves, total)


def solution(mesh):
    lead = lambda rank: P(AXES, *([None] * (rank - 1)))
    placed = (
        lead(2), P(), P(), lead(5), lead(3), lead(3), lead(4), lead(2), lead(2), lead(3), lead(2),
    )
    return jax.shard_map(local, mesh=mesh, in_specs=placed, out_specs=lead(2), check_vma=False)
```

```python
import functools

import jax
import jax.numpy as jnp
from jax import lax
from jax.experimental import pallas as pl
from jax.experimental.pallas import tpu as pltpu
from jax.sharding import PartitionSpec as P

AXES = ("gx", "gy")
LEAD = 8
VMEM = 56 * 1024 * 1024
UNROLL = 32
LOADS = 4
EARLY = 24


def message_kernel(features_ref, requests_ref, counts_ref, out_ref, *, nodes):
    owners, slots = requests_ref.shape
    width = features_ref.shape[2]
    live = jnp.broadcast_to(counts_ref[...], (owners, owners)).T
    lane = lax.broadcasted_iota(jnp.int32, (owners, width), 1)
    rows = []
    for half in range(slots // width):
        at = pl.ds(half * width, width)
        rows.append(jnp.where(lane + half * width < live, requests_ref[:, at] + LEAD, nodes + LEAD))
    digits = [row // width for row in rows] + [row % width for row in rows]
    digits = jnp.stack([digit.astype(jnp.float32) for digit in digits], axis=1)
    out_ref[...] = jnp.concatenate([features_ref[...], digits.astype(jnp.bfloat16)], axis=1)


def build_message(features, requests, counts, owners):
    nodes, width = features.shape
    piece = nodes // owners
    rows = piece + 2 * requests.shape[1] // width
    return pl.pallas_call(
        functools.partial(message_kernel, nodes=nodes),
        out_shape=jax.ShapeDtypeStruct((owners, rows, width), jnp.bfloat16),
        compiler_params=pltpu.CompilerParams(vmem_limit_bytes=VMEM),
        name="build_message",
    )(features.reshape(owners, piece, width), requests, counts)


def gather_kernel(index_ref, features_ref, weight_ref, *refs, half, halves, first_owner):
    out_ref, wide_ref = refs[-2:]
    nodes = features_ref.shape[0]
    owners, tile, width = out_ref.shape
    first = first_owner + pl.program_id(0) * owners

    @pl.when(pl.program_id(0) == 0)
    def _():
        projected = jnp.dot(features_ref[...], weight_ref[...], preferred_element_type=jnp.float32)
        wide_ref[pl.ds(LEAD, nodes), :] = projected.astype(jnp.bfloat16).astype(jnp.float32)
        wide_ref[pl.ds(LEAD + nodes, 8), :] = jnp.zeros((8, width), jnp.float32)

    sublane = lax.broadcasted_iota(jnp.int32, (8, width), 0)
    masks = [sublane == j for j in range(8)]

    def one_owner(owner, carry):
        start = ((first + owner) * halves + half) * tile
        parts = []
        for eight in range(tile // 8):
            rows = None
            for j in range(8):
                at = index_ref[start + eight * 8 + j]
                found = wide_ref[pl.ds(at - j, 8), :]
                rows = found if rows is None else jnp.where(masks[j], found, rows)
            parts.append(rows)
        out_ref[owner] = jnp.concatenate(parts, axis=0).astype(jnp.bfloat16)
        return carry

    lax.fori_loop(0, owners, one_owner, 0)


def gather_rows(wanted, features, weight, half, halves, owners, begin, end, earlier=None, owners_step=8):
    nodes, width = features.shape
    tile = wanted.shape[0] // owners // halves
    first = begin // owners_step
    more = [] if earlier is None else [earlier]
    return pl.pallas_call(
        functools.partial(gather_kernel, half=half, halves=halves, first_owner=begin),
        grid_spec=pltpu.PrefetchScalarGridSpec(
            num_scalar_prefetch=1,
            grid=((end - begin) // owners_step,),
            in_specs=[
                pl.BlockSpec((nodes, width), lambda i, w: (0, 0)),
                pl.BlockSpec((width, width), lambda i, w: (0, 0)),
            ]
            + [pl.BlockSpec(memory_space=pl.ANY) for _ in more],
            out_specs=pl.BlockSpec((owners_step, tile, width), lambda i, w: (first + i, 0, 0)),
            scratch_shapes=[pltpu.VMEM((LEAD + nodes + 8, width), jnp.float32)],
        ),
        out_shape=jax.ShapeDtypeStruct((owners, tile, width), jnp.bfloat16),
        input_output_aliases={3: 0} if more else {},
        compiler_params=pltpu.CompilerParams(vmem_limit_bytes=VMEM),
        name="gather_rows",
    )(wanted, features, weight, *more)


def value_copy(values_ref, held_ref, sems, part):
    size = held_ref.shape[0] // LOADS
    at = pl.ds(part * size, size)
    return pltpu.make_async_copy(values_ref.at[at], held_ref.at[at], sems.at[part])


def dense_kernel(
    rows_ref, cols_ref, source_hbm, values_ref, begin_hbm, total_ref, source_ref, held_ref, begin_ref, sems, value_sems
):
    load_source = pltpu.make_async_copy(source_hbm, source_ref, sems.at[0])
    load_begin = pltpu.make_async_copy(begin_hbm, begin_ref, sems.at[1])
    load_source.start()
    for part in range(LOADS):
        value_copy(values_ref, held_ref, value_sems, part).start()
    load_begin.start()
    total_ref[...] = jnp.zeros_like(total_ref)
    load_source.wait()
    count, tile, _ = held_ref.shape
    size = count // LOADS
    pieces, stripes, piece, _ = source_ref.shape
    per_tile = tile // piece

    def group(step, carry):
        @pl.when(step % (size // UNROLL) == 0)
        def _():
            value_copy(values_ref, held_ref, value_sems, step // (size // UNROLL)).wait()

        stripe = step // (count // stripes // UNROLL)
        for j in range(UNROLL):
            k = step * UNROLL + j
            block = source_ref[pl.ds(cols_ref[k] * per_tile, per_tile), stripe].reshape(tile, tile)
            product = jnp.dot(held_ref[k], block, preferred_element_type=jnp.float32)
            at = pl.ds(pl.multiple_of(rows_ref[k] * tile, tile), tile)
            total_ref[at, :] += product
        return carry

    lax.fori_loop(0, count // UNROLL, group, 0)
    load_begin.wait()
    total_ref[...] += begin_ref[...]


def dense_sum(rows, cols, source, values, begin):
    hbm = pl.BlockSpec(memory_space=pl.ANY)
    return pl.pallas_call(
        dense_kernel,
        grid_spec=pltpu.PrefetchScalarGridSpec(
            num_scalar_prefetch=2,
            grid=(1,),
            in_specs=[hbm] * 3,
            out_specs=pl.BlockSpec(begin.shape, lambda i, r, c: (0, 0)),
            scratch_shapes=[
                pltpu.VMEM(source.shape, jnp.bfloat16),
                pltpu.VMEM(values.shape, jnp.bfloat16),
                pltpu.VMEM(begin.shape, jnp.float32),
                pltpu.SemaphoreType.DMA((2,)),
                pltpu.SemaphoreType.DMA((LOADS,)),
            ],
        ),
        out_shape=jax.ShapeDtypeStruct(begin.shape, jnp.float32),
        compiler_params=pltpu.CompilerParams(vmem_limit_bytes=VMEM),
        name="dense_sum",
    )(rows, cols, source, values, begin)


def sparse_kernel(rows_ref, cols_ref, source_hbm, values_ref, *refs, half, halves, last):
    out_ref, source_ref, held_ref, total_ref, begin_ref, list_ref, sems, value_sems = refs[-8:]
    nodes = out_ref.shape[0]
    count = held_ref.shape[0]
    load_source = pltpu.make_async_copy(source_hbm, source_ref, sems.at[0])
    load_source.start()
    for part in range(LOADS):
        value_copy(values_ref, held_ref, value_sems, part).start()
    if last:
        load_begin = pltpu.make_async_copy(refs[0], begin_ref, sems.at[1])
        load_begin.start()
    total_ref[...] = jnp.zeros_like(total_ref)

    def choose(k, taken):
        list_ref[taken] = k
        return taken + jnp.where(cols_ref[k] % halves == half, 1, 0)

    taken = lax.fori_loop(0, count, choose, 0, unroll=8)
    load_source.wait()
    size = count // LOADS

    def wait_part(part, carry):
        value_copy(values_ref, held_ref, value_sems, part).wait()
        return carry

    def group(step, ready):
        last_k = list_ref[jnp.minimum(step * UNROLL + UNROLL, taken) - 1]
        need = last_k // size + 1
        lax.fori_loop(ready, need, wait_part, 0)
        for j in range(UNROLL):
            entry = step * UNROLL + j
            real = entry < taken
            k = jnp.where(real, list_ref[jnp.minimum(entry, taken - 1)], last_k)
            row = jnp.where(real, rows_ref[k], nodes // 128)
            block = source_ref[cols_ref[k] // halves]
            product = jnp.dot(held_ref[k], block, preferred_element_type=jnp.float32)
            at = pl.ds(pl.multiple_of(row * 128, 128), 128)
            total_ref[at, :] += product
        return jnp.maximum(ready, need)

    ready = lax.fori_loop(0, pl.cdiv(taken, UNROLL), group, 0)
    lax.fori_loop(ready, LOADS, wait_part, 0)
    result = total_ref[pl.ds(0, nodes), :]
    if last:
        load_begin.wait()
        result = jnp.maximum(result + begin_ref[...], 0.0)
    out_ref[...] = result.astype(out_ref.dtype)


def sparse_sum(rows, cols, source, values, nodes, half, halves, begin=None):
    hbm = pl.BlockSpec(memory_space=pl.ANY)
    shape = (nodes, source.shape[-1])
    last = begin is not None
    more = [begin] if last else []
    return pl.pallas_call(
        functools.partial(sparse_kernel, half=half, halves=halves, last=last),
        grid_spec=pltpu.PrefetchScalarGridSpec(
            num_scalar_prefetch=2,
            grid=(1,),
            in_specs=[hbm] * (2 + len(more)),
            out_specs=pl.BlockSpec(shape, lambda i, r, c: (0, 0)),
            scratch_shapes=[
                pltpu.VMEM(source.shape, jnp.bfloat16),
                pltpu.VMEM(values.shape, jnp.bfloat16),
                pltpu.VMEM((nodes + 128, shape[1]), jnp.float32),
                pltpu.VMEM(shape if last else (8, shape[1]), jnp.float32),
                pltpu.SMEM((values.shape[0] + 8,), jnp.int32),
                pltpu.SemaphoreType.DMA((2,)),
                pltpu.SemaphoreType.DMA((LOADS,)),
            ],
        ),
        out_shape=jax.ShapeDtypeStruct(shape, jnp.bfloat16 if last else jnp.float32),
        compiler_params=pltpu.CompilerParams(vmem_limit_bytes=VMEM),
        name="sparse_sum",
    )(rows, cols, source, values, *more)


def local(
    features,
    weight,
    stripe_owner,
    dense_vals,
    dense_rows,
    dense_cols,
    sparse_vals,
    sparse_rows,
    sparse_cols,
    requests,
    counts,
):
    rows_dev, width = features.shape
    tile = dense_vals.shape[-1]
    owners = requests.shape[1]
    slots = requests.shape[2]
    halves = slots // tile
    piece = rows_dev // owners
    message = build_message(features, requests[0], counts, owners)
    message = lax.all_to_all(message, AXES, split_axis=0, concat_axis=0, tiled=True)
    mine = jnp.take(message[:, :piece], stripe_owner, axis=0)
    mine = jnp.dot(mine, weight, preferred_element_type=jnp.float32).astype(jnp.bfloat16)
    stripes = lax.all_gather(mine[None], AXES, axis=0, tiled=True)
    digits = message[:, piece:].astype(jnp.int32).reshape(owners, 2, slots)
    wanted = (digits[:, 0] * 128 + digits[:, 1]).reshape(-1)
    selected = gather_rows(wanted, features, weight, 0, halves, owners, 0, owners)
    if EARLY:
        ahead = gather_rows(wanted, features, weight, 1, halves, owners, 0, EARLY)
        selected, wanted, ahead = lax.optimization_barrier((selected, wanted, ahead))
    else:
        ahead = None
        selected, wanted = lax.optimization_barrier((selected, wanted))
    received = lax.all_to_all(selected, AXES, split_axis=0, concat_axis=0, tiled=True)
    selected = gather_rows(wanted, features, weight, 1, halves, owners, EARLY, owners, ahead)
    total = sparse_sum(sparse_rows[0], sparse_cols[0], received, sparse_vals[0], rows_dev, 0, halves)
    received = lax.all_to_all(selected, AXES, split_axis=0, concat_axis=0, tiled=True)
    total = dense_sum(
        dense_rows.reshape(-1), dense_cols.reshape(-1), stripes, dense_vals.reshape(-1, tile, tile), total
    )
    return sparse_sum(sparse_rows[0], sparse_cols[0], received, sparse_vals[0], rows_dev, 1, halves, total)


def solution(mesh):
    lead = lambda rank: P(AXES, *([None] * (rank - 1)))
    placed = (
        lead(2), P(), P(), lead(5), lead(3), lead(3), lead(4), lead(2), lead(2), lead(3), lead(2),
    )
    return jax.shard_map(local, mesh=mesh, in_specs=placed, out_specs=lead(2), check_vma=False)
```

```python
import functools

import jax
import jax.numpy as jnp
from jax import lax
from jax.experimental import pallas as pl
from jax.experimental.pallas import tpu as pltpu
from jax.sharding import PartitionSpec as P

AXES = ("gx", "gy")
LEAD = 8
VMEM = 56 * 1024 * 1024
VMEM_TILES = 36 * 1024 * 1024
UNROLL = 32
LOADS = 4
EARLY = 32


def in_hbm(array):
    return pltpu.with_memory_space_constraint(array, pltpu.HBM)


def message_kernel(features_ref, requests_ref, counts_ref, out_ref, *, nodes):
    owners, slots = requests_ref.shape
    width = features_ref.shape[2]
    live = jnp.broadcast_to(counts_ref[...], (owners, owners)).T
    lane = lax.broadcasted_iota(jnp.int32, (owners, width), 1)
    rows = []
    for half in range(slots // width):
        at = pl.ds(half * width, width)
        rows.append(jnp.where(lane + half * width < live, requests_ref[:, at] + LEAD, nodes + LEAD))
    digits = [row // width for row in rows] + [row % width for row in rows]
    digits = jnp.stack([digit.astype(jnp.float32) for digit in digits], axis=1)
    out_ref[...] = jnp.concatenate([features_ref[...], digits.astype(jnp.bfloat16)], axis=1)


def build_message(features, requests, counts, owners):
    nodes, width = features.shape
    piece = nodes // owners
    rows = piece + 2 * requests.shape[1] // width
    return pl.pallas_call(
        functools.partial(message_kernel, nodes=nodes),
        out_shape=jax.ShapeDtypeStruct((owners, rows, width), jnp.bfloat16),
        compiler_params=pltpu.CompilerParams(vmem_limit_bytes=VMEM),
        name="build_message",
    )(features.reshape(owners, piece, width), requests, counts)


def gather_kernel(index_ref, features_ref, weight_ref, *refs, half, halves, first_owner):
    out_ref, wide_ref = refs[-2:]
    nodes = features_ref.shape[0]
    owners, tile, width = out_ref.shape
    first = first_owner + pl.program_id(0) * owners

    @pl.when(pl.program_id(0) == 0)
    def _():
        projected = jnp.dot(features_ref[...], weight_ref[...], preferred_element_type=jnp.float32)
        wide_ref[pl.ds(LEAD, nodes), :] = projected.astype(jnp.bfloat16).astype(jnp.float32)
        wide_ref[pl.ds(LEAD + nodes, 8), :] = jnp.zeros((8, width), jnp.float32)

    sublane = lax.broadcasted_iota(jnp.int32, (8, width), 0)
    masks = [sublane == j for j in range(8)]

    def one_owner(owner, carry):
        start = ((first + owner) * halves + half) * tile
        parts = []
        for eight in range(tile // 8):
            rows = None
            for j in range(8):
                at = index_ref[start + eight * 8 + j]
                found = wide_ref[pl.ds(at - j, 8), :]
                rows = found if rows is None else jnp.where(masks[j], found, rows)
            parts.append(rows)
        out_ref[owner] = jnp.concatenate(parts, axis=0).astype(jnp.bfloat16)
        return carry

    lax.fori_loop(0, owners, one_owner, 0)


def gather_rows(wanted, features, weight, half, halves, owners, begin, end, earlier=None, owners_step=8):
    nodes, width = features.shape
    tile = wanted.shape[0] // owners // halves
    first = begin // owners_step
    more = [] if earlier is None else [earlier]
    return pl.pallas_call(
        functools.partial(gather_kernel, half=half, halves=halves, first_owner=begin),
        grid_spec=pltpu.PrefetchScalarGridSpec(
            num_scalar_prefetch=1,
            grid=((end - begin) // owners_step,),
            in_specs=[
                pl.BlockSpec((nodes, width), lambda i, w: (0, 0)),
                pl.BlockSpec((width, width), lambda i, w: (0, 0)),
            ]
            + [pl.BlockSpec(memory_space=pl.ANY) for _ in more],
            out_specs=pl.BlockSpec((owners_step, tile, width), lambda i, w: (first + i, 0, 0)),
            scratch_shapes=[pltpu.VMEM((LEAD + nodes + 8, width), jnp.float32)],
        ),
        out_shape=jax.ShapeDtypeStruct((owners, tile, width), jnp.bfloat16),
        input_output_aliases={3: 0} if more else {},
        compiler_params=pltpu.CompilerParams(vmem_limit_bytes=VMEM),
        name="gather_rows",
    )(wanted, features, weight, *more)


def value_copy(values_ref, held_ref, sems, part):
    size = held_ref.shape[0] // LOADS
    at = pl.ds(part * size, size)
    return pltpu.make_async_copy(values_ref.at[at], held_ref.at[at], sems.at[part])


def dense_kernel(
    rows_ref, cols_ref, source_hbm, values_ref, begin_hbm, total_ref, source_ref, held_ref, begin_ref, sems, value_sems
):
    load_source = pltpu.make_async_copy(source_hbm, source_ref, sems.at[0])
    load_begin = pltpu.make_async_copy(begin_hbm, begin_ref, sems.at[1])
    load_source.start()
    for part in range(LOADS):
        value_copy(values_ref, held_ref, value_sems, part).start()
    load_begin.start()
    total_ref[...] = jnp.zeros_like(total_ref)
    load_source.wait()
    count, tile, _ = held_ref.shape
    size = count // LOADS
    pieces, stripes, piece, _ = source_ref.shape
    per_tile = tile // piece

    def group(step, carry):
        @pl.when(step % (size // UNROLL) == 0)
        def _():
            value_copy(values_ref, held_ref, value_sems, step // (size // UNROLL)).wait()

        stripe = step // (count // stripes // UNROLL)
        for j in range(UNROLL):
            k = step * UNROLL + j
            block = source_ref[pl.ds(cols_ref[k] * per_tile, per_tile), stripe].reshape(tile, tile)
            product = jnp.dot(held_ref[k], block, preferred_element_type=jnp.float32)
            at = pl.ds(pl.multiple_of(rows_ref[k] * tile, tile), tile)
            total_ref[at, :] += product
        return carry

    lax.fori_loop(0, count // UNROLL, group, 0)
    load_begin.wait()
    total_ref[...] += begin_ref[...]


def dense_sum(rows, cols, source, values, begin):
    hbm = pl.BlockSpec(memory_space=pl.ANY)
    return pl.pallas_call(
        dense_kernel,
        grid_spec=pltpu.PrefetchScalarGridSpec(
            num_scalar_prefetch=2,
            grid=(1,),
            in_specs=[hbm] * 3,
            out_specs=pl.BlockSpec(begin.shape, lambda i, r, c: (0, 0)),
            scratch_shapes=[
                pltpu.VMEM(source.shape, jnp.bfloat16),
                pltpu.VMEM(values.shape, jnp.bfloat16),
                pltpu.VMEM(begin.shape, jnp.float32),
                pltpu.SemaphoreType.DMA((2,)),
                pltpu.SemaphoreType.DMA((LOADS,)),
            ],
        ),
        out_shape=jax.ShapeDtypeStruct(begin.shape, jnp.float32),
        compiler_params=pltpu.CompilerParams(vmem_limit_bytes=VMEM_TILES),
        name="dense_sum",
    )(rows, cols, in_hbm(source), in_hbm(values), in_hbm(begin))


def choose_half(cols_ref, list_ref, count, half, halves):
    def choose(k, taken):
        list_ref[taken] = k
        return taken + jnp.where(cols_ref[k] % halves == half, 1, 0)

    return lax.fori_loop(0, count, choose, 0, unroll=8)


def first_kernel(
    rows_ref, cols_ref, source_hbm, values_ref, out_ref, picked_ref, later_ref, source_ref, held_ref, total_ref, list_ref,
    source_sem, value_sems,
):
    nodes = out_ref.shape[0]
    count = held_ref.shape[0]
    load_source = pltpu.make_async_copy(source_hbm, source_ref, source_sem)
    load_source.start()
    for part in range(LOADS):
        value_copy(values_ref, held_ref, value_sems, part).start()
    total_ref[...] = jnp.zeros_like(total_ref)
    taken = choose_half(cols_ref, list_ref, count, 0, 2)
    later = choose_half(cols_ref, later_ref, count, 1, 2)
    later_ref[count] = later
    load_source.wait()
    for part in range(LOADS):
        value_copy(values_ref, held_ref, value_sems, part).wait()

    def group(step, carry):
        for j in range(UNROLL):
            entry = step * UNROLL + j
            k = list_ref[jnp.minimum(entry, taken - 1)]
            row = jnp.where(entry < taken, rows_ref[k], nodes // 128)
            product = jnp.dot(held_ref[k], source_ref[cols_ref[k] // 2], preferred_element_type=jnp.float32)
            at = pl.ds(pl.multiple_of(row * 128, 128), 128)
            total_ref[at, :] += product
        return carry

    lax.fori_loop(0, pl.cdiv(taken, UNROLL), group, 0)

    def pick(entry, carry):
        picked_ref[entry] = held_ref[later_ref[entry]]
        return carry

    lax.fori_loop(0, later, pick, 0)
    out_ref[...] = total_ref[pl.ds(0, nodes), :]


def first_sum(rows, cols, source, values, nodes):
    hbm = pl.BlockSpec(memory_space=pl.ANY)
    shape = (nodes, source.shape[-1])
    count = values.shape[0]
    return pl.pallas_call(
        first_kernel,
        grid_spec=pltpu.PrefetchScalarGridSpec(
            num_scalar_prefetch=2,
            grid=(1,),
            in_specs=[hbm] * 2,
            out_specs=[
                pl.BlockSpec(shape, lambda i, r, c: (0, 0)),
                pl.BlockSpec(values.shape, lambda i, r, c: (0, 0, 0)),
                pl.BlockSpec(memory_space=pltpu.SMEM),
            ],
            scratch_shapes=[
                pltpu.VMEM(source.shape, jnp.bfloat16),
                pltpu.VMEM(values.shape, jnp.bfloat16),
                pltpu.VMEM((nodes + 128, shape[1]), jnp.float32),
                pltpu.SMEM((count + 8,), jnp.int32),
                pltpu.SemaphoreType.DMA,
                pltpu.SemaphoreType.DMA((LOADS,)),
            ],
        ),
        out_shape=[
            jax.ShapeDtypeStruct(shape, jnp.float32),
            jax.ShapeDtypeStruct(values.shape, jnp.bfloat16),
            jax.ShapeDtypeStruct((count + 8,), jnp.int32),
        ],
        compiler_params=pltpu.CompilerParams(vmem_limit_bytes=VMEM_TILES),
        name="first_sum",
    )(rows, cols, in_hbm(source), in_hbm(values))


def last_kernel(
    rows_ref, cols_ref, list_ref, source_ref, begin_ref, values_ref, out_ref, held_ref, total_ref, value_sems
):
    nodes = begin_ref.shape[0]
    count = held_ref.shape[0]
    taken = list_ref[count]

    def load_values(part):
        at = pl.ds(part * UNROLL, UNROLL)
        return pltpu.make_async_copy(values_ref.at[at], held_ref.at[at], value_sems.at[part])

    for part in range(count // UNROLL):

        @pl.when(part * UNROLL < taken)
        def _():
            load_values(part).start()

    total_ref[pl.ds(0, nodes), :] = begin_ref[...]
    total_ref[pl.ds(nodes, 128), :] = jnp.zeros((128, total_ref.shape[1]), jnp.float32)

    def group(step, carry):
        load_values(step).wait()
        for j in range(UNROLL):
            entry = jnp.minimum(step * UNROLL + j, taken - 1)
            k = list_ref[entry]
            row = jnp.where(step * UNROLL + j < taken, rows_ref[k], nodes // 128)
            product = jnp.dot(held_ref[entry], source_ref[cols_ref[k] // 2], preferred_element_type=jnp.float32)
            at = pl.ds(pl.multiple_of(row * 128, 128), 128)
            total_ref[at, :] += product
        return carry

    lax.fori_loop(0, pl.cdiv(taken, UNROLL), group, 0)
    out_ref[...] = jnp.maximum(total_ref[pl.ds(0, nodes), :], 0.0).astype(jnp.bfloat16)


def last_sum(rows, cols, listed, source, values, begin):
    nodes, width = begin.shape
    smem = pl.BlockSpec(memory_space=pltpu.SMEM)
    vmem = pl.BlockSpec(memory_space=pltpu.VMEM)
    source, begin = (pltpu.with_memory_space_constraint(a, pltpu.VMEM) for a in (source, begin))
    return pl.pallas_call(
        last_kernel,
        in_specs=[smem] * 3 + [vmem] * 2 + [pl.BlockSpec(memory_space=pltpu.HBM)],
        out_specs=vmem,
        scratch_shapes=[
            pltpu.VMEM(values.shape, jnp.bfloat16),
            pltpu.VMEM((nodes + 128, width), jnp.float32),
            pltpu.SemaphoreType.DMA((values.shape[0] // UNROLL,)),
        ],
        out_shape=jax.ShapeDtypeStruct(begin.shape, jnp.bfloat16),
        compiler_params=pltpu.CompilerParams(vmem_limit_bytes=VMEM_TILES),
        name="last_sum",
    )(rows, cols, listed, source, begin, pltpu.with_memory_space_constraint(values, pltpu.HBM))


def local(
    features,
    weight,
    stripe_owner,
    dense_vals,
    dense_rows,
    dense_cols,
    sparse_vals,
    sparse_rows,
    sparse_cols,
    requests,
    counts,
):
    rows_dev, width = features.shape
    tile = dense_vals.shape[-1]
    owners = requests.shape[1]
    slots = requests.shape[2]
    halves = slots // tile
    piece = rows_dev // owners
    message = build_message(features, requests[0], counts, owners)
    message = lax.all_to_all(message, AXES, split_axis=0, concat_axis=0, tiled=True)
    mine = jnp.take(message[:, :piece], stripe_owner, axis=0)
    mine = jnp.dot(mine, weight, preferred_element_type=jnp.float32).astype(jnp.bfloat16)
    stripes = lax.all_gather(mine[None], AXES, axis=0, tiled=True)
    digits = message[:, piece:].astype(jnp.int32).reshape(owners, 2, slots)
    wanted = (digits[:, 0] * 128 + digits[:, 1]).reshape(-1)
    selected = gather_rows(wanted, features, weight, 0, halves, owners, 0, owners)
    if EARLY:
        ahead = gather_rows(wanted, features, weight, 1, halves, owners, 0, EARLY)
        selected, wanted, ahead = lax.optimization_barrier((selected, wanted, ahead))
    else:
        ahead = None
        selected, wanted = lax.optimization_barrier((selected, wanted))
    received = lax.all_to_all(selected, AXES, split_axis=0, concat_axis=0, tiled=True)
    selected = gather_rows(wanted, features, weight, 1, halves, owners, EARLY, owners, ahead)
    total, picked, listed = first_sum(sparse_rows[0], sparse_cols[0], received, sparse_vals[0], rows_dev)
    received = lax.all_to_all(selected, AXES, split_axis=0, concat_axis=0, tiled=True)
    total = dense_sum(
        dense_rows.reshape(-1), dense_cols.reshape(-1), stripes, dense_vals.reshape(-1, tile, tile), total
    )
    return last_sum(sparse_rows[0], sparse_cols[0], listed, received, picked, total)


def solution(mesh):
    lead = lambda rank: P(AXES, *([None] * (rank - 1)))
    placed = (
        lead(2), P(), P(), lead(5), lead(3), lead(3), lead(4), lead(2), lead(2), lead(3), lead(2),
    )
    return jax.shard_map(local, mesh=mesh, in_specs=placed, out_specs=lead(2), check_vma=False)
```

```python
import functools

import jax
import jax.numpy as jnp
from jax import lax
from jax.experimental import pallas as pl
from jax.experimental.pallas import tpu as pltpu
from jax.sharding import PartitionSpec as P

AXES = ("gx", "gy")
LEAD = 8
VMEM = 56 * 1024 * 1024
VMEM_TILES = 36 * 1024 * 1024
UNROLL = 32
LOADS = 4
EARLY = 32


def in_hbm(array):
    return pltpu.with_memory_space_constraint(array, pltpu.HBM)


def message_kernel(features_ref, requests_ref, counts_ref, out_ref, *, nodes):
    owners, slots = requests_ref.shape
    width = features_ref.shape[2]
    live = jnp.broadcast_to(counts_ref[...], (owners, owners)).T
    lane = lax.broadcasted_iota(jnp.int32, (owners, width), 1)
    rows = []
    for half in range(slots // width):
        at = pl.ds(half * width, width)
        rows.append(jnp.where(lane + half * width < live, requests_ref[:, at] + LEAD, nodes + LEAD))
    digits = [row // width for row in rows] + [row % width for row in rows]
    digits = jnp.stack([digit.astype(jnp.float32) for digit in digits], axis=1)
    out_ref[...] = jnp.concatenate([features_ref[...], digits.astype(jnp.bfloat16)], axis=1)


def build_message(features, requests, counts, owners):
    nodes, width = features.shape
    piece = nodes // owners
    rows = piece + 2 * requests.shape[1] // width
    return pl.pallas_call(
        functools.partial(message_kernel, nodes=nodes),
        out_shape=jax.ShapeDtypeStruct((owners, rows, width), jnp.bfloat16),
        compiler_params=pltpu.CompilerParams(vmem_limit_bytes=VMEM),
        name="build_message",
    )(features.reshape(owners, piece, width), requests, counts)


def gather_kernel(index_ref, features_ref, weight_ref, *refs, half, halves, first_owner):
    out_ref, wide_ref = refs[-2:]
    nodes = features_ref.shape[0]
    owners, tile, width = out_ref.shape
    first = first_owner + pl.program_id(0) * owners

    @pl.when(pl.program_id(0) == 0)
    def _():
        projected = jnp.dot(features_ref[...], weight_ref[...], preferred_element_type=jnp.float32)
        wide_ref[pl.ds(LEAD, nodes), :] = projected.astype(jnp.bfloat16).astype(jnp.float32)
        wide_ref[pl.ds(LEAD + nodes, 8), :] = jnp.zeros((8, width), jnp.float32)

    sublane = lax.broadcasted_iota(jnp.int32, (8, width), 0)
    masks = [sublane == j for j in range(8)]

    def one_owner(owner, carry):
        start = ((first + owner) * halves + half) * tile
        parts = []
        for eight in range(tile // 8):
            rows = None
            for j in range(8):
                at = index_ref[start + eight * 8 + j]
                found = wide_ref[pl.ds(at - j, 8), :]
                rows = found if rows is None else jnp.where(masks[j], found, rows)
            parts.append(rows)
        out_ref[owner] = jnp.concatenate(parts, axis=0).astype(jnp.bfloat16)
        return carry

    lax.fori_loop(0, owners, one_owner, 0)


def gather_rows(wanted, features, weight, half, halves, owners, begin, end, earlier=None, owners_step=8):
    nodes, width = features.shape
    tile = wanted.shape[0] // owners // halves
    first = begin // owners_step
    more = [] if earlier is None else [earlier]
    return pl.pallas_call(
        functools.partial(gather_kernel, half=half, halves=halves, first_owner=begin),
        grid_spec=pltpu.PrefetchScalarGridSpec(
            num_scalar_prefetch=1,
            grid=((end - begin) // owners_step,),
            in_specs=[
                pl.BlockSpec((nodes, width), lambda i, w: (0, 0)),
                pl.BlockSpec((width, width), lambda i, w: (0, 0)),
            ]
            + [pl.BlockSpec(memory_space=pl.ANY) for _ in more],
            out_specs=pl.BlockSpec((owners_step, tile, width), lambda i, w: (first + i, 0, 0)),
            scratch_shapes=[pltpu.VMEM((LEAD + nodes + 8, width), jnp.float32)],
        ),
        out_shape=jax.ShapeDtypeStruct((owners, tile, width), jnp.bfloat16),
        input_output_aliases={3: 0} if more else {},
        compiler_params=pltpu.CompilerParams(vmem_limit_bytes=VMEM),
        name="gather_rows",
    )(wanted, features, weight, *more)


def value_copy(values_ref, held_ref, sems, part):
    size = held_ref.shape[0] // LOADS
    at = pl.ds(part * size, size)
    return pltpu.make_async_copy(values_ref.at[at], held_ref.at[at], sems.at[part])


def dense_kernel(
    rows_ref, cols_ref, source_hbm, values_ref, begin_hbm, total_ref, source_ref, held_ref, begin_ref, sems, value_sems
):
    load_source = pltpu.make_async_copy(source_hbm, source_ref, sems.at[0])
    load_begin = pltpu.make_async_copy(begin_hbm, begin_ref, sems.at[1])
    load_source.start()
    for part in range(LOADS):
        value_copy(values_ref, held_ref, value_sems, part).start()
    load_begin.start()
    total_ref[...] = jnp.zeros_like(total_ref)
    load_source.wait()
    count, tile, _ = held_ref.shape
    size = count // LOADS
    pieces, stripes, piece, _ = source_ref.shape
    per_tile = tile // piece

    def group(step, carry):
        @pl.when(step % (size // UNROLL) == 0)
        def _():
            value_copy(values_ref, held_ref, value_sems, step // (size // UNROLL)).wait()

        stripe = step // (count // stripes // UNROLL)
        for j in range(UNROLL):
            k = step * UNROLL + j
            block = source_ref[pl.ds(cols_ref[k] * per_tile, per_tile), stripe].reshape(tile, tile)
            product = jnp.dot(held_ref[k], block, preferred_element_type=jnp.float32)
            at = pl.ds(pl.multiple_of(rows_ref[k] * tile, tile), tile)
            total_ref[at, :] += product
        return carry

    lax.fori_loop(0, count // UNROLL, group, 0)
    load_begin.wait()
    total_ref[...] += begin_ref[...]


def dense_sum(rows, cols, source, values, begin):
    hbm = pl.BlockSpec(memory_space=pl.ANY)
    return pl.pallas_call(
        dense_kernel,
        grid_spec=pltpu.PrefetchScalarGridSpec(
            num_scalar_prefetch=2,
            grid=(1,),
            in_specs=[hbm] * 3,
            out_specs=pl.BlockSpec(begin.shape, lambda i, r, c: (0, 0)),
            scratch_shapes=[
                pltpu.VMEM(source.shape, jnp.bfloat16),
                pltpu.VMEM(values.shape, jnp.bfloat16),
                pltpu.VMEM(begin.shape, jnp.float32),
                pltpu.SemaphoreType.DMA((2,)),
                pltpu.SemaphoreType.DMA((LOADS,)),
            ],
        ),
        out_shape=jax.ShapeDtypeStruct(begin.shape, jnp.float32),
        compiler_params=pltpu.CompilerParams(vmem_limit_bytes=VMEM_TILES),
        name="dense_sum",
    )(rows, cols, in_hbm(source), in_hbm(values), in_hbm(begin))


def choose_half(cols_ref, list_ref, count, half, halves):
    def choose(k, taken):
        list_ref[taken] = k
        return taken + jnp.where(cols_ref[k] % halves == half, 1, 0)

    return lax.fori_loop(0, count, choose, 0, unroll=8)


def first_kernel(
    rows_ref, cols_ref, source_hbm, values_ref, out_ref, picked_ref, later_ref, source_ref, held_ref, total_ref, list_ref,
    source_sem, value_sems,
):
    nodes = out_ref.shape[0]
    count = held_ref.shape[0]
    load_source = pltpu.make_async_copy(source_hbm, source_ref, source_sem)
    load_source.start()
    for part in range(LOADS):
        value_copy(values_ref, held_ref, value_sems, part).start()
    total_ref[...] = jnp.zeros_like(total_ref)
    taken = choose_half(cols_ref, list_ref, count, 0, 2)
    later = choose_half(cols_ref, later_ref, count, 1, 2)
    later_ref[count] = later
    load_source.wait()
    for part in range(LOADS):
        value_copy(values_ref, held_ref, value_sems, part).wait()

    def group(step, carry):
        for j in range(UNROLL):
            entry = step * UNROLL + j
            k = list_ref[jnp.minimum(entry, taken - 1)]
            row = jnp.where(entry < taken, rows_ref[k], nodes // 128)
            product = jnp.dot(held_ref[k], source_ref[cols_ref[k] // 2], preferred_element_type=jnp.float32)
            at = pl.ds(pl.multiple_of(row * 128, 128), 128)
            total_ref[at, :] += product
        return carry

    lax.fori_loop(0, pl.cdiv(taken, UNROLL), group, 0)

    def pick(entry, carry):
        picked_ref[entry] = held_ref[later_ref[entry]]
        return carry

    lax.fori_loop(0, later, pick, 0)
    out_ref[...] = total_ref[pl.ds(0, nodes), :]


def first_sum(rows, cols, source, values, nodes):
    hbm = pl.BlockSpec(memory_space=pl.ANY)
    shape = (nodes, source.shape[-1])
    count = values.shape[0]
    return pl.pallas_call(
        first_kernel,
        grid_spec=pltpu.PrefetchScalarGridSpec(
            num_scalar_prefetch=2,
            grid=(1,),
            in_specs=[hbm] * 2,
            out_specs=[
                pl.BlockSpec(shape, lambda i, r, c: (0, 0)),
                pl.BlockSpec(values.shape, lambda i, r, c: (0, 0, 0)),
                pl.BlockSpec(memory_space=pltpu.SMEM),
            ],
            scratch_shapes=[
                pltpu.VMEM(source.shape, jnp.bfloat16),
                pltpu.VMEM(values.shape, jnp.bfloat16),
                pltpu.VMEM((nodes + 128, shape[1]), jnp.float32),
                pltpu.SMEM((count + 8,), jnp.int32),
                pltpu.SemaphoreType.DMA,
                pltpu.SemaphoreType.DMA((LOADS,)),
            ],
        ),
        out_shape=[
            jax.ShapeDtypeStruct(shape, jnp.float32),
            jax.ShapeDtypeStruct(values.shape, jnp.bfloat16),
            jax.ShapeDtypeStruct((count + 8,), jnp.int32),
        ],
        compiler_params=pltpu.CompilerParams(vmem_limit_bytes=VMEM_TILES),
        name="first_sum",
    )(rows, cols, in_hbm(source), in_hbm(values))


def last_kernel(
    rows_ref, cols_ref, list_ref, source_ref, begin_ref, values_ref, out_ref, held_ref, total_ref, value_sems
):
    nodes = begin_ref.shape[0]
    count = held_ref.shape[0]
    taken = list_ref[count]

    def load_values(part):
        at = pl.ds(part * UNROLL, UNROLL)
        return pltpu.make_async_copy(values_ref.at[at], held_ref.at[at], value_sems.at[part])

    def start_values(part):
        @pl.when(part * UNROLL < taken)
        def _():
            load_values(part).start()

    start_values(0)
    start_values(1)
    total_ref[pl.ds(0, nodes), :] = begin_ref[...]
    total_ref[pl.ds(nodes, 128), :] = jnp.zeros((128, total_ref.shape[1]), jnp.float32)

    def group(step, carry):
        load_values(step).wait()
        start_values(step + 2)
        for j in range(UNROLL):
            entry = jnp.minimum(step * UNROLL + j, taken - 1)
            k = list_ref[entry]
            row = jnp.where(step * UNROLL + j < taken, rows_ref[k], nodes // 128)
            product = jnp.dot(held_ref[entry], source_ref[cols_ref[k] // 2], preferred_element_type=jnp.float32)
            at = pl.ds(pl.multiple_of(row * 128, 128), 128)
            total_ref[at, :] += product
        return carry

    lax.fori_loop(0, pl.cdiv(taken, UNROLL), group, 0)
    out_ref[...] = jnp.maximum(total_ref[pl.ds(0, nodes), :], 0.0).astype(jnp.bfloat16)


def last_sum(rows, cols, listed, source, values, begin):
    nodes, width = begin.shape
    smem = pl.BlockSpec(memory_space=pltpu.SMEM)
    vmem = pl.BlockSpec(memory_space=pltpu.VMEM)
    source, begin = (pltpu.with_memory_space_constraint(a, pltpu.VMEM) for a in (source, begin))
    return pl.pallas_call(
        last_kernel,
        in_specs=[smem] * 3 + [vmem] * 2 + [pl.BlockSpec(memory_space=pltpu.HBM)],
        out_specs=vmem,
        scratch_shapes=[
            pltpu.VMEM(values.shape, jnp.bfloat16),
            pltpu.VMEM((nodes + 128, width), jnp.float32),
            pltpu.SemaphoreType.DMA((values.shape[0] // UNROLL,)),
        ],
        out_shape=jax.ShapeDtypeStruct(begin.shape, jnp.bfloat16),
        compiler_params=pltpu.CompilerParams(vmem_limit_bytes=VMEM_TILES),
        name="last_sum",
    )(rows, cols, listed, source, begin, pltpu.with_memory_space_constraint(values, pltpu.HBM))


def local(
    features,
    weight,
    stripe_owner,
    dense_vals,
    dense_rows,
    dense_cols,
    sparse_vals,
    sparse_rows,
    sparse_cols,
    requests,
    counts,
):
    rows_dev, width = features.shape
    tile = dense_vals.shape[-1]
    owners = requests.shape[1]
    slots = requests.shape[2]
    halves = slots // tile
    piece = rows_dev // owners
    message = build_message(features, requests[0], counts, owners)
    message = lax.all_to_all(message, AXES, split_axis=0, concat_axis=0, tiled=True)
    mine = jnp.take(message[:, :piece], stripe_owner, axis=0)
    mine = jnp.dot(mine, weight, preferred_element_type=jnp.float32).astype(jnp.bfloat16)
    stripes = lax.all_gather(mine[None], AXES, axis=0, tiled=True)
    digits = message[:, piece:].astype(jnp.int32).reshape(owners, 2, slots)
    wanted = (digits[:, 0] * 128 + digits[:, 1]).reshape(-1)
    selected = gather_rows(wanted, features, weight, 0, halves, owners, 0, owners)
    if EARLY:
        ahead = gather_rows(wanted, features, weight, 1, halves, owners, 0, EARLY)
        selected, wanted, ahead = lax.optimization_barrier((selected, wanted, ahead))
    else:
        ahead = None
        selected, wanted = lax.optimization_barrier((selected, wanted))
    received = lax.all_to_all(selected, AXES, split_axis=0, concat_axis=0, tiled=True)
    selected = gather_rows(wanted, features, weight, 1, halves, owners, EARLY, owners, ahead)
    total, picked, listed = first_sum(sparse_rows[0], sparse_cols[0], received, sparse_vals[0], rows_dev)
    received = lax.all_to_all(selected, AXES, split_axis=0, concat_axis=0, tiled=True)
    total = dense_sum(
        dense_rows.reshape(-1), dense_cols.reshape(-1), stripes, dense_vals.reshape(-1, tile, tile), total
    )
    return last_sum(sparse_rows[0], sparse_cols[0], listed, received, picked, total)


def solution(mesh):
    lead = lambda rank: P(AXES, *([None] * (rank - 1)))
    placed = (
        lead(2), P(), P(), lead(5), lead(3), lead(3), lead(4), lead(2), lead(2), lead(3), lead(2),
    )
    return jax.shard_map(local, mesh=mesh, in_specs=placed, out_specs=lead(2), check_vma=False)
```
